256 devices in a mesh: dp: 32 (over z, y_hi, core), group: 8 (over y_lo, x).
Axes of the slice: x: 4, y: 4 (y_hi: 2, y_lo: 2; y = y_hi * 2 + y_lo), z: 8, core: 2. Of those that a mesh axis runs over, the one named last changes fastest.
Arguments:
- feats: bfloat16 [1536, 320, 128], P(('dp', 'group')), may hold values from -6 to 6
- utt_lengths: int32 [32, 8, 4], P('dp', 'group'), may hold values from 0 to 768, as said below
- offsets: int32 [32, 8], P('dp', 'group'), may hold values from 0 to 24, as said below
- conv_kernel: bfloat16 [128, 40], replicated, may hold values from -1 to 1
- conv_bias: float32 [128], replicated, may hold values from -3 to 3
- lin_weight: bfloat16 [1024, 1536], replicated, may hold values from -0.1875 to 0.1875
- lin_bias: float32 [1536], replicated, may hold values from -3 to 3
- ln_gain: float32 [2, 1536], replicated, may hold values from 0.1 to 1.9
- w_in: bfloat16 [2, 1536, 3072], P(None, 'dp'), may hold values from -0.15625 to 0.15625
- dw_weight: float32 [2, 32, 1536], replicated, may hold values from -1 to 1
- bn_scale: float32 [2, 1536], replicated, may hold values from 0.1 to 1.9
- bn_shift: float32 [2, 1536], replicated, may hold values from -3 to 3
- w_out: bfloat16 [2, 1536, 1536], P(None, 'dp'), may hold values from -0.15625 to 0.15625
Outputs:
- frames: bfloat16 [98304, 1536], P(('dp', 'group'))
The draws below stay inside these ranges and needn't reach their ends.
Inputs may be any that keep to these rules, and one draw needn't show every extreme that they name: `utt_lengths`: A device's utterances lie end to end from frame 0 of its block slots; the lengths of one device sum to 128 times a whole number of 0 to 6, those of one group to 3072; in every group one device holds 6 blocks, all in its first utterance, and one holds none. offsets[i, e] is the sum of the block counts (lengths over 128) of members 0 to e - 1 of the same group.
All inputs are finite; a program needn't handle non-finite values.
Results may differ from the reference program's by a relative error of at most 0.018.
Values may be sent and summed in bfloat16 or wider, within the bound.
No kernel may reach another device: no remote copies, remote signals or barrier semaphores. Data moves between devices by JAX's collectives and lax.ppermute only.
A program may use at most 128 MiB of HBM per device.

```python
import jax
import jax.numpy as jnp
from jax import lax

D = 1536
MEL = 80
SUB_CH = 128
FK = 10
TSTRIDE = 4
BINS = 8
KER = 32
HW = 16
LAYERS = 2
BLK = 128
UTT = 4
BAL = 3
NS = 6
N_DP = 32
N_GROUP = 8


def block_counts(key):
    pair_key, swap_key, full_key = jax.random.split(key, 3)
    pair_count = N_GROUP // 2
    pair_share = jax.random.randint(pair_key, (N_DP, pair_count), 0, 2 * BAL + 1)
    chosen = jax.random.randint(full_key, (N_DP, 1), 0, pair_count)
    pair_share = jnp.where(jnp.arange(pair_count)[None, :] == chosen, 2 * BAL, pair_share)
    paired = jnp.stack([pair_share, 2 * BAL - pair_share], axis=-1).reshape(N_DP, N_GROUP)
    device_order = jax.vmap(lambda row_key: jax.random.permutation(row_key, N_GROUP))(jax.random.split(swap_key, N_DP))
    first_order = device_order[0]
    empty_slot = (2 * chosen[0, 0] + 1).astype(first_order.dtype)
    empty_place = jnp.argmax(first_order == empty_slot)
    last_entry = first_order[N_GROUP - 1]
    first_order = first_order.at[empty_place].set(last_entry).at[N_GROUP - 1].set(empty_slot)
    device_order = device_order.at[0].set(first_order)
    return jnp.take_along_axis(paired, device_order, axis=1).astype(jnp.int32)


def draw_utt_lengths(key, part):
    counts = block_counts(key)
    key = jax.random.fold_in(key, 7)
    total_frames = counts * BLK
    cuts = jax.random.randint(key, (N_DP, N_GROUP, UTT - 1), 0, total_frames[..., None] + 1)
    cuts = jnp.where((counts == 2 * BAL)[..., None], total_frames[..., None], cuts)
    cuts = jnp.sort(cuts, axis=-1)
    edges = jnp.concatenate([jnp.zeros((N_DP, N_GROUP, 1), jnp.int32), cuts.astype(jnp.int32), total_frames[..., None]], axis=-1)
    return jnp.diff(edges, axis=-1).astype(jnp.int32)


def draw_offsets(key, part):
    counts = block_counts(key)
    return (jnp.cumsum(counts, axis=1) - counts).astype(jnp.int32)


def steps_of(rng, shape, cuts, least, top_value):
    factor_of = 1.0
    for dim, shards_of in cuts:
        steps = jax.random.uniform(jax.random.fold_in(jax.random.fold_in(rng, 6), dim), (shards_of,), jnp.float32, least / len(cuts), top_value / len(cuts))
        factor_of = factor_of * jnp.repeat(jnp.exp(steps), shape[dim] // shards_of).reshape((-1,) + (1,) * (len(shape) - 1 - dim))
    return factor_of


def gaussian(rng, dims, deviation, limit, pieces=(), kind=jnp.bfloat16):
    array = deviation * jax.random.normal(rng, dims, jnp.float32)
    if pieces:
        array = array * steps_of(rng, dims, pieces, -0.22, 0.18)
    return jnp.clip(array, -limit, limit).astype(kind)


def setup_inputs(seed: int = 0) -> dict:
    arg_keys = jax.random.split(jax.random.key(seed), 14)
    feats = gaussian(arg_keys[0], (N_DP * N_GROUP * NS, TSTRIDE * MEL, BLK), 1.0, 6.0, ((0, 256),))
    utt_lengths = draw_utt_lengths(jax.random.fold_in(arg_keys[13], 71), 0)
    offsets = draw_offsets(jax.random.fold_in(arg_keys[13], 71), 0)
    conv_kernel = gaussian(arg_keys[3], (SUB_CH, TSTRIDE * FK), (TSTRIDE * FK) ** -0.5, 1.0)
    conv_bias = gaussian(arg_keys[4], (SUB_CH,), 0.5, 3.0, (), jnp.float32)
    lin_weight = gaussian(arg_keys[5], (SUB_CH * BINS, D), (SUB_CH * BINS) ** -0.5, 0.1875)
    lin_bias = gaussian(arg_keys[6], (D,), 0.5, 3.0, (), jnp.float32)
    ln_gain = jnp.clip(1.0 + 0.18 * jax.random.normal(arg_keys[7], (LAYERS, D), jnp.float32), 0.1, 1.9)
    w_in = gaussian(arg_keys[8], (LAYERS, D, 2 * D), D ** -0.5, 0.15625, ((1, 32),))
    dw_weight = gaussian(arg_keys[9], (LAYERS, KER, D), KER ** -0.5, 1.0, (), jnp.float32)
    bn_scale = jnp.clip(1.0 + 0.18 * jax.random.normal(arg_keys[10], (LAYERS, D), jnp.float32), 0.1, 1.9)
    bn_shift = gaussian(arg_keys[11], (LAYERS, D), 0.5, 3.0, (), jnp.float32)
    w_out = gaussian(arg_keys[12], (LAYERS, D, D), D ** -0.5, 0.15625, ((1, 32),))
    return dict(feats=feats, utt_lengths=utt_lengths, offsets=offsets, conv_kernel=conv_kernel, conv_bias=conv_bias, lin_weight=lin_weight, lin_bias=lin_bias, ln_gain=ln_gain, w_in=w_in, dw_weight=dw_weight, bn_scale=bn_scale, bn_shift=bn_shift, w_out=w_out)


eps_norm = 1e-05

def layer_norm(frames, gain):
    wide = frames.astype(jnp.float32)
    centre = wide - lax.optimization_barrier(jnp.mean(wide, axis=-1, keepdims=True))
    spread = lax.optimization_barrier(jnp.mean(centre * centre, axis=-1, keepdims=True))
    return (centre * lax.rsqrt(spread + eps_norm) * gain).astype(jnp.bfloat16)

def subsample(blocks, conv_kernel, conv_bias, lin_weight, lin_bias):
    count_blocks = blocks.shape[0]
    stacked = blocks.reshape(count_blocks, TSTRIDE, BINS, FK, BLK).astype(jnp.float32)
    kernel = conv_kernel.reshape(SUB_CH, TSTRIDE, FK).astype(jnp.float32)
    conv_out = jnp.einsum('cim,bifmt->bcft', kernel, stacked)
    hidden = jax.nn.relu(conv_out + conv_bias[None, :, None, None]).astype(jnp.bfloat16)
    hidden = hidden.reshape(count_blocks, SUB_CH * BINS, BLK).astype(jnp.float32)
    frames = jnp.einsum('bkt,kd->btd', hidden, lin_weight.astype(jnp.float32))
    return (frames + lin_bias).astype(jnp.bfloat16).reshape(count_blocks * BLK, D)

def conv_module(frames, labels, gain, weight_in, taps, scale, shift, weight_out):
    normed = layer_norm(frames, gain)
    projected = jnp.dot(normed, weight_in, preferred_element_type=jnp.float32)
    gated = (projected[:, :D] * jax.nn.sigmoid(projected[:, D:])).astype(jnp.bfloat16)
    count_rows = frames.shape[0]
    padded = jnp.pad(gated.astype(jnp.float32), ((HW, HW), (0, 0)))
    padded_labels = jnp.pad(labels, (HW, HW), constant_values=-1)
    depthwise = jnp.zeros((count_rows, D), jnp.float32)
    for tap_index in range(KER):
        window = padded[tap_index:tap_index + count_rows] * taps[tap_index]
        keep_tap = (padded_labels[tap_index:tap_index + count_rows] == labels)[:, None]
        depthwise = depthwise + jnp.where(keep_tap, window, 0.0)
    scaled = depthwise * scale + shift
    active = (scaled * jax.nn.sigmoid(scaled)).astype(jnp.bfloat16)
    update = jnp.dot(active, weight_out, preferred_element_type=jnp.float32)
    return (frames.astype(jnp.float32) + update).astype(jnp.bfloat16)

def reference(feats, utt_lengths, offsets, conv_kernel, conv_bias, lin_weight, lin_bias, ln_gain, w_in, dw_weight, bn_scale, bn_shift, w_out):
    raw_rows = feats.reshape(N_DP, N_GROUP, NS, TSTRIDE * MEL, BLK)

    def one_group(operands):
        group_feats, group_lengths, starts = operands
        starts = starts.astype(jnp.int32)
        counts = (lax.optimization_barrier(jnp.sum(group_lengths, axis=1)) // BLK).astype(jnp.int32)
        position = jnp.arange(N_GROUP * BAL, dtype=jnp.int32)
        inside = ((starts[None, :] <= position[:, None]) & (position[:, None] < (starts + counts)[None, :])).astype(jnp.int32)
        source = lax.optimization_barrier(jnp.sum(inside * jnp.arange(N_GROUP, dtype=jnp.int32)[None, :], axis=1)).astype(jnp.int32)
        source_start = lax.optimization_barrier(jnp.sum(inside * starts[None, :], axis=1)).astype(jnp.int32)
        blocks = group_feats[source, (position - source_start).astype(jnp.int32)]
        frames = subsample(blocks, conv_kernel, conv_bias, lin_weight, lin_bias)
        bounds = (starts[:, None] * BLK + jnp.cumsum(group_lengths, axis=1).astype(jnp.int32)).reshape(-1).astype(jnp.int32)
        where_at = jnp.arange(N_GROUP * BAL * BLK, dtype=jnp.int32)
        labels = lax.optimization_barrier(jnp.sum((bounds[None, :] <= where_at[:, None]).astype(jnp.int32), axis=1)).astype(jnp.int32)
        for layer_index in range(LAYERS):
            frames = conv_module(frames, labels, ln_gain[layer_index], w_in[layer_index], dw_weight[layer_index], bn_scale[layer_index], bn_shift[layer_index], w_out[layer_index])
        return frames.reshape(BAL, N_GROUP, BLK, D).transpose(1, 0, 2, 3).reshape(N_GROUP * BAL * BLK, D)
    result = lax.map(one_group, (raw_rows, utt_lengths, offsets))
    return result.reshape(N_DP * N_GROUP * BAL * BLK, D)
```

```python
import functools

import jax
import jax.numpy as jnp
from jax import lax
from jax.experimental import pallas as pl
from jax.experimental.pallas import tpu as pltpu
from jax.sharding import Mesh
from jax.sharding import PartitionSpec as P

FK = 10
TSTRIDE = 4
eps_norm = 1e-05

AXES = ("z", "yh", "c", "yl", "x")
SIZES = (8, 2, 2, 2, 4)
DP = ("z", "yh", "c")
GROUP = ("yl", "x")
LANES = 128
VMEM_LIMIT = 56 * 1024 * 1024


def layer_norm(wide, gain):
    centre = wide - jnp.mean(wide, axis=-1, keepdims=True)
    spread = jnp.mean(centre * centre, axis=-1, keepdims=True)
    return (centre * lax.rsqrt(spread + eps_norm) * gain).astype(jnp.bfloat16)


def ring(axis, step):
    count = lax.axis_size(axis)
    return [(i, (i + step) % count) for i in range(count)]


def core_swap(block):
    return lax.ppermute(block, "c", [(0, 1), (1, 0)])


def y_swap(block):
    return lax.ppermute(block, ("yh", "yl"), [(i, 3 - i) for i in range(4)])


def glu_kernel(at_ref, own_ref, other_ref, *refs):
    blocks, (out_own, out_other, weight, sems) = refs[:5], refs[5:]
    at = at_ref[0]
    half = weight.shape[1] // 2
    targets = [
        weight.at[at],
        weight.at[lax.rem(at + 1, 4)],
        weight.at[lax.rem(at + 3, 4)],
        weight.at[lax.rem(at + 2, 4), pl.ds(0, half)],
        weight.at[lax.rem(at + 2, 4), pl.ds(half, half)],
    ]
    copies = [
        pltpu.make_async_copy(block, target, sems.at[slot])
        for slot, (block, target) in enumerate(zip(blocks, targets))
    ]
    for copy in copies:
        copy.start()
    for copy in copies:
        copy.wait()
    cols = weight.shape[-1]
    for frames_ref, out_ref in ((own_ref, out_own), (other_ref, out_other)):
        frames = frames_ref[...]
        for half in range(2):
            a = jnp.dot(frames, weight[half], preferred_element_type=jnp.float32)
            b = jnp.dot(frames, weight[2 + half], preferred_element_type=jnp.float32)
            out_ref[:, pl.ds(half * cols, cols)] = (a * jax.nn.sigmoid(b)).astype(jnp.bfloat16)


def gated_units(at, own, other, blocks):
    rows, width = own.shape
    cols = blocks[0].shape[1]
    vmem = pl.BlockSpec(memory_space=pltpu.VMEM)
    return pl.pallas_call(
        glu_kernel,
        out_shape=[jax.ShapeDtypeStruct((rows, 2 * cols), jnp.bfloat16)] * 2,
        in_specs=[pl.BlockSpec(memory_space=pltpu.SMEM), vmem, vmem]
        + [pl.BlockSpec(memory_space=pl.ANY)] * 5,
        out_specs=[vmem, vmem],
        scratch_shapes=[
            pltpu.VMEM((4, width, cols), jnp.bfloat16),
            pltpu.SemaphoreType.DMA((5,)),
        ],
        compiler_params=pltpu.CompilerParams(vmem_limit_bytes=VMEM_LIMIT),
        cost_estimate=pl.CostEstimate(
            flops=2 * 2 * rows * width * 4 * cols, bytes_accessed=8 * 10**6, transcendentals=0
        ),
        name="gated_units",
    )(at, own, other, *blocks)


def channel_kernel(run, core_ref, all_ref, out_ref):
    width, kept = all_ref.shape[1], out_ref.shape[1]
    row = lax.broadcasted_iota(jnp.int32, (width, kept), 0)
    made = lax.broadcasted_iota(jnp.int32, (width, kept), 1)
    taken = (2 * (made // run) + core_ref[0]) * run + made % run
    pick = jnp.where(row == taken, 1.0, 0.0).astype(jnp.bfloat16)
    rest = all_ref[...]
    total = jnp.zeros(out_ref.shape, jnp.float32)
    for _ in range(3):
        piece = rest.astype(jnp.bfloat16)
        total = total + jnp.dot(piece, pick, preferred_element_type=jnp.float32)
        rest = rest - piece.astype(jnp.float32)
    out_ref[...] = total


def channels(core, array, run):
    rows, width = array.shape
    vmem = pl.BlockSpec(memory_space=pltpu.VMEM)
    return pl.pallas_call(
        functools.partial(channel_kernel, run),
        out_shape=jax.ShapeDtypeStruct((rows, width // 2), jnp.float32),
        in_specs=[pl.BlockSpec(memory_space=pltpu.SMEM), vmem],
        out_specs=vmem,
        compiler_params=pltpu.CompilerParams(vmem_limit_bytes=VMEM_LIMIT),
        name="channels",
    )(core, array)


def tail_kernel(taps, rim, row_of, glu_ref, low_ref, high_ref, label_ref, small_ref, weight_ref, out_ref, padded, act):
    rows, width = glu_ref.shape
    padded[0:rim] = low_ref[0].astype(jnp.float32)
    padded[rim : rim + rows] = glu_ref[...].astype(jnp.float32)
    padded[rim + rows : rows + 2 * rim] = high_ref[0].astype(jnp.float32)
    group = 32

    def lane_tile(tile, carry):
        lanes = pl.ds(pl.multiple_of(tile * LANES, LANES), LANES)
        scale, shift = small_ref[pl.ds(row_of[1], 1), lanes], small_ref[pl.ds(row_of[2], 1), lanes]
        for start in range(0, rows, group):
            centre = label_ref[0, rim + start : rim + start + group, :]
            total = jnp.zeros((group, LANES), jnp.float32)
            for tap in range(taps):
                window = padded[start + tap : start + tap + group, lanes]
                keep = label_ref[0, start + tap : start + tap + group, :] == centre
                total = total + jnp.where(keep, window * small_ref[pl.ds(row_of[0] + tap, 1), lanes], 0.0)
            scaled = total * scale + shift
            act[start : start + group, lanes] = (scaled * jax.nn.sigmoid(scaled)).astype(
                jnp.bfloat16
            )
        return carry

    lax.fori_loop(0, width // LANES, lane_tile, 0)
    out_ref[...] = jnp.dot(
        act[...], weight_ref[...], preferred_element_type=jnp.float32
    ).astype(out_ref.dtype)


def module_tail(first, glu, low, high, labels, taps, row_of, small, weight, kind):
    rim, width = low.shape[1:]
    rows = labels.shape[1] - 2 * rim
    count = glu.shape[0] // rows
    out_width = weight.shape[1]
    whole = lambda *shape: pl.BlockSpec(shape, lambda i: (0,) * len(shape))
    return pl.pallas_call(
        functools.partial(tail_kernel, taps, rim, row_of),
        grid=(count,),
        out_shape=jax.ShapeDtypeStruct((count * rows, out_width), kind),
        in_specs=[
            pl.BlockSpec((rows, width), lambda i: (i, 0)),
            pl.BlockSpec((1, rim, width), lambda i: (first + i, 0, 0)),
            pl.BlockSpec((1, rim, width), lambda i: (first + i, 0, 0)),
            pl.BlockSpec((1, rows + 2 * rim, LANES), lambda i: (first + i, 0, 0)),
            whole(*small.shape),
            whole(width, out_width),
        ],
        out_specs=pl.BlockSpec((rows, out_width), lambda i: (i, 0)),
        scratch_shapes=[
            pltpu.VMEM((rows + 2 * rim, width), jnp.float32),
            pltpu.VMEM((rows, width), jnp.bfloat16),
        ],
        compiler_params=pltpu.CompilerParams(vmem_limit_bytes=VMEM_LIMIT),
        cost_estimate=pl.CostEstimate(
            flops=2 * count * rows * width * (out_width + 64 * taps),
            bytes_accessed=4 * 10**6,
            transcendentals=0,
        ),
        name="module_tail",
    )(glu, low, high, labels, small, weight)


def local(
    feats,
    utt_lengths,
    offsets,
    conv_kernel,
    conv_bias,
    lin_weight,
    lin_bias,
    ln_gain,
    w_in,
    dw_weight,
    bn_scale,
    bn_shift,
    w_out,
):
    groups = lax.axis_size("yl") * lax.axis_size("x")
    member = lax.axis_index(GROUP)
    core = lax.axis_index("c")
    x_at = lax.axis_index("x")
    yh_at = lax.axis_index("yh")
    own_slots = feats.shape[0]
    blk_rows = feats.shape[2]
    slot_count = own_slots // 2
    capacity = (own_slots + groups - 1) // groups
    model_width = lin_weight.shape[1]
    layer_count = ln_gain.shape[0]
    kernel_taps = dw_weight.shape[1]
    rim_width = kernel_taps // 2
    shard = w_in.shape[1]
    half_width = model_width // 2
    y_at = 2 * yh_at + lax.axis_index("yl")

    quarter = 2 * model_width // 4
    cut = lambda layer, at: lax.dynamic_slice_in_dim(w_in[layer], at * quarter, quarter, axis=1)
    cuts = jnp.concatenate([cut(0, x_at), cut(1, y_at), cut(1, 3 - y_at)], axis=0)
    made = jnp.arange(quarter, dtype=jnp.int32)
    side, run = made // (quarter // 2), made % (quarter // 2)
    taken = (2 * (run // shard) + jnp.bitwise_xor(side, core)) * shard + run % shard
    pick = (made[:, None] == taken[None, :]).astype(jnp.bfloat16)
    sorted_cuts = jnp.dot(cuts, pick, preferred_element_type=jnp.float32).astype(jnp.bfloat16)
    sorted_cuts = sorted_cuts.reshape(3, shard, 2, quarter // 2)
    mine, sent = sorted_cuts[:, :, 0], sorted_cuts[:, :, 1]
    from_core = core_swap(sent[:2])
    from_y = y_swap(mine[0::2])
    from_both = lax.ppermute(sent[0::2], ("yh", "c", "yl"), [(i, 7 - i) for i in range(8)])

    def ordered(at, first, second):
        return jnp.where(
            at == 0,
            jnp.concatenate([first, second], axis=1),
            jnp.concatenate([second, first], axis=1),
        )

    both = ordered(
        yh_at, ordered(core, mine[:2], from_core), ordered(core, from_y, from_both)
    )

    feats, utt_lengths, offsets, both = lax.optimization_barrier(
        (feats, utt_lengths, offsets, both)
    )
    columns = lax.all_gather(both, "z", axis=1, tiled=True)

    weight_in = []
    middle = model_width // 2
    for layer, axes in enumerate(("x", ("yh", "yl"))):
        held = columns[layer]
        left = lax.ppermute(held, axes, ring(axes, 1))
        right = lax.ppermute(held, axes, ring(axes, -1))
        low_part = lax.ppermute(left[:middle], axes, ring(axes, 1))
        high_part = lax.ppermute(right[middle:], axes, ring(axes, -1))
        weight_in.append([held, right, left, low_part, high_part])
    places = [x_at.reshape(1).astype(jnp.int32), y_at.reshape(1).astype(jnp.int32)]

    header = jnp.concatenate([offsets.reshape(1), utt_lengths.reshape(-1)])[None, :]
    table = lax.all_gather(header, ("c",) + GROUP, axis=0, tiled=True)
    table = table.reshape(2, groups, -1)
    own_table = jnp.where(core == 0, table[0], table[1])
    starts = own_table[:, 0]
    counts = jnp.sum(own_table[:, 1:], axis=1) // blk_rows
    own_start = offsets.reshape(())
    destined = jnp.arange(groups, dtype=jnp.int32)[:, None]
    rounds = jnp.arange(capacity, dtype=jnp.int32)[None, :]
    chosen = jnp.mod(destined - own_start, groups) + rounds * groups
    outgoing = feats[jnp.clip(chosen, 0, own_slots - 1)]
    outgoing, w_out = lax.optimization_barrier((outgoing, w_out))

    rows_out = ordered(yh_at, w_out, y_swap(w_out))
    weight_out = [
        lax.all_gather(rows_out[layer], "z", axis=0, tiled=True) for layer in range(layer_count)
    ]

    incoming = lax.all_to_all(outgoing, GROUP, split_axis=0, concat_axis=0, tiled=True)
    position = jnp.arange(slot_count, dtype=jnp.int32) * groups + member
    inside = (
        (starts[None, :] <= position[:, None]) & (position[:, None] < (starts + counts)[None, :])
    ).astype(jnp.int32)
    source = jnp.sum(inside * jnp.arange(groups, dtype=jnp.int32)[None, :], axis=1)
    source_start = jnp.sum(inside * starts[None, :], axis=1)
    blocks = incoming[source, (position - source_start) // groups]

    kernel = conv_kernel.reshape(conv_kernel.shape[0], TSTRIDE, FK)
    stacked = blocks.reshape(slot_count, TSTRIDE, -1, FK, blk_rows)
    conv_out = jnp.einsum("cim,bifmt->bcft", kernel, stacked, preferred_element_type=jnp.float32)
    hidden = jax.nn.relu(conv_out + conv_bias[None, :, None, None]).astype(jnp.bfloat16)
    hidden = hidden.reshape(slot_count, -1, blk_rows)
    frames = jnp.einsum("bkt,kd->btd", hidden, lin_weight, preferred_element_type=jnp.float32)
    frames = (frames + lin_bias).astype(jnp.bfloat16).reshape(slot_count * blk_rows, model_width)

    wide = frames.astype(jnp.float32)
    normed = layer_norm(wide, ln_gain[0])
    normed, columns_done, dw_weight = lax.optimization_barrier((normed, weight_in[0][2], dw_weight))
    weight_in[0][2] = columns_done
    other = core_swap(normed)

    extent = groups * slot_count * blk_rows
    offset_rows = jnp.arange(blk_rows + 2 * rim_width, dtype=jnp.int32) - rim_width
    where_at = (position * blk_rows)[:, None] + offset_rows[None, :]

    def labels_of(one):
        bounds = (one[:, :1] * blk_rows + jnp.cumsum(one[:, 1:], axis=1)).reshape(-1)
        found = jnp.sum((bounds[None, None, :] <= where_at[:, :, None]).astype(jnp.int32), axis=-1)
        return jnp.where((where_at >= 0) & (where_at < extent), found, -1)

    labels = jnp.concatenate([labels_of(table[core]), labels_of(table[1 - core])], axis=0)
    labels = jnp.broadcast_to(labels[:, :, None], labels.shape + (LANES,))

    small = jnp.concatenate([dw_weight.reshape(-1, model_width), bn_scale, bn_shift], axis=0)
    small = channels(core.reshape(1).astype(jnp.int32), small, shard)
    tap_rows = layer_count * kernel_taps

    for layer in range(layer_count):
        if layer:
            normed = layer_norm(wide, ln_gain[layer])
            other = core_swap(normed)
        if layer == 0:
            other, labels, small, weight_in = lax.optimization_barrier(
                (other, labels, small, weight_in)
            )
        own_blocks = normed.reshape(slot_count, blk_rows, model_width)
        other_blocks = other.reshape(slot_count, blk_rows, model_width)
        edge = lambda part: jnp.concatenate([own_blocks[:, part], other_blocks[:, part]]).reshape(
            -1, model_width
        )
        ends, begins = gated_units(
            places[layer],
            edge(slice(blk_rows - rim_width, blk_rows)),
            edge(slice(0, rim_width)),
            weight_in[layer],
        )
        low = lax.ppermute(ends, GROUP, ring(GROUP, 1))
        high = lax.ppermute(begins, GROUP, ring(GROUP, -1))
        glu = gated_units(places[layer], normed, other, weight_in[layer])
        low = low.reshape(2, slot_count, rim_width, half_width)
        high = high.reshape(2, slot_count, rim_width, half_width)
        low = jnp.where(
            member == 0,
            jnp.concatenate([jnp.zeros_like(low[:, :1]), low[:, :-1]], axis=1),
            low,
        ).reshape(2 * slot_count, rim_width, half_width)
        high = jnp.where(
            member == groups - 1,
            jnp.concatenate([high[:, 1:], jnp.zeros_like(high[:, :1])], axis=1),
            high,
        ).reshape(2 * slot_count, rim_width, half_width)
        row_of = (layer * kernel_taps, tap_rows + layer, tap_rows + layer_count + layer)
        tail = lambda part, kind: module_tail(
            part * slot_count, glu[part], low, high, labels, kernel_taps, row_of, small,
            weight_out[layer], kind,
        )
        theirs = core_swap(tail(1, jnp.bfloat16))
        mine = tail(0, jnp.float32)
        update = mine + theirs.astype(jnp.float32)
        frames = (wide + update).astype(jnp.bfloat16)
        wide = frames.astype(jnp.float32)
    return frames


def solution(mesh):
    physical = Mesh(mesh.devices.reshape(SIZES), AXES)
    in_specs = (
        P(DP + GROUP, None, None),
        P(DP, GROUP, None),
        P(DP, GROUP),
        P(),
        P(),
        P(),
        P(),
        P(),
        P(None, DP, None),
        P(),
        P(),
        P(),
        P(None, DP, None),
    )
    out_specs = P(DP + GROUP, None)
    return jax.shard_map(
        local, mesh=physical, in_specs=in_specs, out_specs=out_specs, check_vma=False
    )
```

```python
import functools

import jax
import jax.numpy as jnp
from jax import lax
from jax.experimental import pallas as pl
from jax.experimental.pallas import tpu as pltpu
from jax.sharding import Mesh
from jax.sharding import PartitionSpec as P

FK = 10
TSTRIDE = 4
eps_norm = 1e-05

AXES = ("z", "yh", "c", "yl", "x")
SIZES = (8, 2, 2, 2, 4)
DP = ("z", "yh", "c")
GROUP = ("yl", "x")
LANES = 128
VMEM_LIMIT = 56 * 1024 * 1024
SMALL = pl.CostEstimate(flops=1000, bytes_accessed=1000, transcendentals=0)


def layer_norm(wide, gain):
    centre = wide - jnp.mean(wide, axis=-1, keepdims=True)
    spread = jnp.mean(centre * centre, axis=-1, keepdims=True)
    return (centre * lax.rsqrt(spread + eps_norm) * gain).astype(jnp.bfloat16)


def ring(axis, step):
    count = lax.axis_size(axis)
    return [(i, (i + step) % count) for i in range(count)]


def core_swap(block):
    return lax.ppermute(block, "c", [(0, 1), (1, 0)])


def y_swap(block):
    return lax.ppermute(block, ("yh", "yl"), [(i, 3 - i) for i in range(4)])


def glu_kernel(rim, blk, step, at_ref, own_ref, other_ref, *refs):
    weights, (out_ref, low_ref, high_ref) = refs[:-3], refs[-3:]
    values_first = lax.rem(at_ref[0] + step, 4) < 2
    rows = out_ref.shape[0] // 2
    rim_rows = low_ref.shape[0] // 2

    def product(frames):
        first = jnp.dot(frames, weights[0][...], preferred_element_type=jnp.float32)
        second, depth = 0.0, 0
        for weight in weights[1:]:
            deep = weight.shape[0]
            second = second + jnp.dot(
                frames[:, depth : depth + deep], weight[...], preferred_element_type=jnp.float32
            )
            depth += deep
        a = jnp.where(values_first, first, second)
        b = jnp.where(values_first, second, first)
        return (a * jax.nn.sigmoid(b)).astype(jnp.bfloat16)

    for part, frames_ref in enumerate((own_ref, other_ref)):
        gated = product(frames_ref[...])
        out_ref[part * rows : (part + 1) * rows] = gated[:rows]
        if frames_ref.shape[0] > rows:
            place = slice(part * rim_rows, (part + 1) * rim_rows)
            low_ref[place] = gated[rows : rows + rim_rows]
            high_ref[place] = gated[rows + rim_rows :]
        else:
            for block in range(rows // blk):
                place = part * rim_rows + block * rim
                low_ref[place : place + rim] = gated[(block + 1) * blk - rim : (block + 1) * blk]
                high_ref[place : place + rim] = gated[block * blk : block * blk + rim]


def gated_units(layer, step, rim, blk, slots, at, own, other, weights):
    given, width = own.shape
    cols = weights[0].shape[2]
    rows, rim_rows = slots * blk, slots * rim
    whole = lambda *shape: pl.BlockSpec(shape, lambda i: (0,) * len(shape))
    return pl.pallas_call(
        functools.partial(glu_kernel, rim, blk, step),
        grid=(1,),
        out_shape=[
            jax.ShapeDtypeStruct((2 * count, cols), jnp.bfloat16)
            for count in (rows, rim_rows, rim_rows)
        ],
        in_specs=[pl.BlockSpec(memory_space=pltpu.SMEM), whole(given, width), whole(given, width)]
        + [pl.BlockSpec((None,) + w.shape[1:], lambda i: (layer, 0, 0)) for w in weights],
        out_specs=[whole(2 * rows, cols), whole(2 * rim_rows, cols), whole(2 * rim_rows, cols)],
        compiler_params=pltpu.CompilerParams(vmem_limit_bytes=VMEM_LIMIT),
        cost_estimate=SMALL,
        name="gated_units",
    )(at, own, other, *weights)


def channel_kernel(run, core_ref, all_ref, out_ref):
    width, kept = all_ref.shape[1], out_ref.shape[1]
    row = lax.broadcasted_iota(jnp.int32, (width, kept), 0)
    made = lax.broadcasted_iota(jnp.int32, (width, kept), 1)
    taken = (2 * (made // run) + core_ref[0]) * run + made % run
    pick = jnp.where(row == taken, 1.0, 0.0).astype(jnp.bfloat16)
    rest = all_ref[...]
    total = jnp.zeros(out_ref.shape, jnp.float32)
    for _ in range(3):
        piece = rest.astype(jnp.bfloat16)
        total = total + jnp.dot(piece, pick, preferred_element_type=jnp.float32)
        rest = rest - piece.astype(jnp.float32)
    out_ref[...] = total


def channels(core, array, run):
    rows, width = array.shape
    vmem = pl.BlockSpec(memory_space=pltpu.VMEM)
    return pl.pallas_call(
        functools.partial(channel_kernel, run),
        out_shape=jax.ShapeDtypeStruct((rows, width // 2), jnp.float32),
        in_specs=[pl.BlockSpec(memory_space=pltpu.SMEM), vmem],
        out_specs=vmem,
        compiler_params=pltpu.CompilerParams(vmem_limit_bytes=VMEM_LIMIT),
        name="channels",
    )(core, array)


def depthwise(taps, rim, row_of, base, glu_ref, low_ref, high_ref, label_ref, small_ref, padded, store):
    rows, width = glu_ref.shape
    tiles = width // LANES
    for tile in range(tiles):
        lanes = slice(tile * LANES, (tile + 1) * LANES)
        padded[tile, 0:rim] = low_ref[0, :, lanes].astype(jnp.float32)
        padded[tile, rim : rim + rows] = glu_ref[:, lanes].astype(jnp.float32)
        padded[tile, rim + rows : rows + 2 * rim] = high_ref[0, :, lanes].astype(jnp.float32)
    group = 32
    offset = [pl.ds(pl.multiple_of(base + tile * LANES, LANES), LANES) for tile in range(tiles)]
    for start in range(0, rows, group):
        centre = label_ref[0, rim + start : rim + start + group, :]
        totals = [jnp.zeros((group, LANES), jnp.float32)] * tiles
        for tap in range(taps):
            keep = label_ref[0, start + tap : start + tap + group, :] == centre
            for tile in range(tiles):
                window = padded[tile, start + tap : start + tap + group]
                term = window * small_ref[pl.ds(row_of[0] + tap, 1), offset[tile]]
                totals[tile] = totals[tile] + jnp.where(keep, term, 0.0)
        for tile in range(tiles):
            scale = small_ref[pl.ds(row_of[1], 1), offset[tile]]
            shift = small_ref[pl.ds(row_of[2], 1), offset[tile]]
            scaled = totals[tile] * scale + shift
            store(start, group, tile, (scaled * jax.nn.sigmoid(scaled)).astype(jnp.bfloat16))


def depthwise_kernel(taps, rim, row_of, step, at_ref, glu_ref, low_ref, high_ref, label_ref, small_ref, out_ref, padded):
    base = lax.rem(at_ref[0] + step, 2) * glu_ref.shape[1]

    def store(start, group, tile, value):
        out_ref[start : start + group, tile * LANES : (tile + 1) * LANES] = value

    depthwise(
        taps, rim, row_of, base, glu_ref, low_ref, high_ref, label_ref, small_ref, padded, store
    )


def tail_kernel(taps, rim, row_of, step, at_ref, glu_ref, low_ref, high_ref, label_ref, small_ref, done_ref, weight_ref, out_ref, padded, act):
    width = glu_ref.shape[1]
    half = lax.rem(at_ref[0] + step, 2)
    base = half * width

    def store(start, group, tile, value):
        act[start : start + group, tile * LANES : (tile + 1) * LANES] = value

    depthwise(
        taps, rim, row_of, base, glu_ref, low_ref, high_ref, label_ref, small_ref, padded, store
    )
    done_rows = pl.ds(pl.multiple_of((1 - half) * width, width), width)
    here_rows = pl.ds(pl.multiple_of(base, width), width)
    out_ref[...] = (
        jnp.dot(done_ref[...], weight_ref[done_rows, :], preferred_element_type=jnp.float32)
        + jnp.dot(act[...], weight_ref[here_rows, :], preferred_element_type=jnp.float32)
    ).astype(out_ref.dtype)


def depthwise_call(first, count, taps, row_of, step, at, glu, low, high, labels, small, rest=None, kind=None):
    rim, width = low.shape[1:]
    rows = labels.shape[1] - 2 * rim
    whole = lambda *shape: pl.BlockSpec(shape, lambda i: (0,) * len(shape))
    in_specs = [
        pl.BlockSpec(memory_space=pltpu.SMEM),
        pl.BlockSpec((rows, width), lambda i: (first + i, 0)),
        pl.BlockSpec((1, rim, width), lambda i: (first + i, 0, 0)),
        pl.BlockSpec((1, rim, width), lambda i: (first + i, 0, 0)),
        pl.BlockSpec((1, rows + 2 * rim, LANES), lambda i: (first + i, 0, 0)),
        whole(*small.shape),
    ]
    scratch = [pltpu.VMEM((width // LANES, rows + 2 * rim, LANES), jnp.float32)]
    if rest is None:
        body, out_width, kind, more = depthwise_kernel, width, jnp.bfloat16, ()
    else:
        done, weight = rest
        body, out_width, more = tail_kernel, weight.shape[1], (done, weight)
        in_specs += [pl.BlockSpec((rows, width), lambda i: (first + i, 0)), whole(*weight.shape)]
        scratch += [pltpu.VMEM((rows, width), jnp.bfloat16)]
    return pl.pallas_call(
        functools.partial(body, taps, rim, row_of, step),
        grid=(count,),
        out_shape=jax.ShapeDtypeStruct((count * rows, out_width), kind),
        in_specs=in_specs,
        out_specs=pl.BlockSpec((rows, out_width), lambda i: (i, 0)),
        scratch_shapes=scratch,
        compiler_params=pltpu.CompilerParams(vmem_limit_bytes=VMEM_LIMIT),
        cost_estimate=SMALL,
        name="depthwise" if rest is None else "module_tail",
    )(at, glu, low, high, labels, small, *more)


def local(
    feats,
    utt_lengths,
    offsets,
    conv_kernel,
    conv_bias,
    lin_weight,
    lin_bias,
    ln_gain,
    w_in,
    dw_weight,
    bn_scale,
    bn_shift,
    w_out,
):
    groups = lax.axis_size("yl") * lax.axis_size("x")
    member = lax.axis_index(GROUP)
    core = lax.axis_index("c")
    x_at = lax.axis_index("x")
    yh_at = lax.axis_index("yh")
    own_slots = feats.shape[0]
    blk_rows = feats.shape[2]
    slot_count = own_slots // 2
    capacity = (own_slots + groups - 1) // groups
    model_width = lin_weight.shape[1]
    layer_count = ln_gain.shape[0]
    kernel_taps = dw_weight.shape[1]
    rim_width = kernel_taps // 2
    shard = w_in.shape[1]
    half_width = model_width // 2
    y_at = 2 * yh_at + lax.axis_index("yl")

    quarter = 2 * model_width // 4
    place, place_y = [lax.rem(x_at + 2 * (y % 2), 4) for y in (y_at, 3 - y_at)]
    cut = lambda at: lax.dynamic_slice_in_dim(w_in, at * quarter, quarter, axis=2)
    cuts = jnp.concatenate([cut(place), cut(place_y)], axis=0).reshape(-1, quarter)
    made = jnp.arange(quarter, dtype=jnp.int32)
    side, run = made // (quarter // 2), made % (quarter // 2)
    taken = (2 * (run // shard) + jnp.bitwise_xor(side, core)) * shard + run % shard
    pick = (made[:, None] == taken[None, :]).astype(jnp.bfloat16)
    sorted_cuts = jnp.dot(cuts, pick, preferred_element_type=jnp.float32).astype(jnp.bfloat16)
    sorted_cuts = sorted_cuts.reshape(4, shard, 2, quarter // 2)
    mine, sent = sorted_cuts[:, :, 0], sorted_cuts[:, :, 1]
    from_core = core_swap(sent[:2])
    from_y = y_swap(mine[2:])
    from_both = lax.ppermute(sent[2:], ("yh", "c", "yl"), [(i, 7 - i) for i in range(8)])

    def ordered(at, first, second):
        return jnp.where(
            at == 0,
            jnp.concatenate([first, second], axis=1),
            jnp.concatenate([second, first], axis=1),
        )

    both = ordered(
        yh_at, ordered(core, mine[:2], from_core), ordered(core, from_y, from_both)
    )

    feats, utt_lengths, offsets, both = lax.optimization_barrier(
        (feats, utt_lengths, offsets, both)
    )
    swapped = y_swap(w_out)
    columns = lax.all_gather(both, "z", axis=1, tiled=True)

    header = jnp.concatenate([offsets.reshape(1), utt_lengths.reshape(-1)])
    fields = header.shape[0]
    digits = jnp.concatenate([header // 256, header % 256]).astype(feats.dtype)
    head_rows = jnp.zeros((16, blk_rows), feats.dtype).at[0, : 2 * fields].set(digits)
    own_start = offsets.reshape(())
    destined = jnp.arange(groups, dtype=jnp.int32)[:, None]
    rounds = jnp.arange(capacity, dtype=jnp.int32)[None, :]
    chosen = jnp.mod(destined - own_start, groups) + rounds * groups
    outgoing = jnp.concatenate(
        [
            feats[jnp.clip(chosen, 0, own_slots - 1)],
            jnp.broadcast_to(head_rows, chosen.shape + head_rows.shape),
        ],
        axis=2,
    )
    rows_out = ordered(yh_at, w_out, swapped)
    weight_out = [
        lax.all_gather(rows_out[layer], "z", axis=0, tiled=True) for layer in range(layer_count)
    ]

    incoming = lax.all_to_all(outgoing, GROUP, split_axis=0, concat_axis=0, tiled=True)
    raw_rows = feats.shape[1]
    digits = incoming[:, 0, raw_rows, : 2 * fields].astype(jnp.int32)
    own_table = digits[:, :fields] * 256 + digits[:, fields:]
    sib_table = core_swap(own_table)
    starts = own_table[:, 0]
    counts = jnp.sum(own_table[:, 1:], axis=1) // blk_rows
    position = jnp.arange(slot_count, dtype=jnp.int32) * groups + member
    inside = (
        (starts[None, :] <= position[:, None]) & (position[:, None] < (starts + counts)[None, :])
    ).astype(jnp.int32)
    source = jnp.sum(inside * jnp.arange(groups, dtype=jnp.int32)[None, :], axis=1)
    source_start = jnp.sum(inside * starts[None, :], axis=1)
    blocks = incoming[source, (position - source_start) // groups][:, :raw_rows]

    kernel = conv_kernel.reshape(conv_kernel.shape[0], TSTRIDE, FK)
    stacked = blocks.reshape(slot_count, TSTRIDE, -1, FK, blk_rows)
    conv_out = jnp.einsum("cim,bifmt->bcft", kernel, stacked, preferred_element_type=jnp.float32)
    hidden = jax.nn.relu(conv_out + conv_bias[None, :, None, None]).astype(jnp.bfloat16)
    hidden = hidden.reshape(slot_count, -1, blk_rows)
    frames = jnp.einsum("bkt,kd->btd", hidden, lin_weight, preferred_element_type=jnp.float32)
    frames = (frames + lin_bias).astype(jnp.bfloat16).reshape(slot_count * blk_rows, model_width)

    wide = frames.astype(jnp.float32)
    normed = layer_norm(wide, ln_gain[0])

    def rims(last, first, parts):
        low = lax.ppermute(last, GROUP, ring(GROUP, 1)).reshape(parts, slot_count, rim_width, -1)
        high = lax.ppermute(first, GROUP, ring(GROUP, -1)).reshape(parts, slot_count, rim_width, -1)
        low = jnp.where(
            member == 0,
            jnp.concatenate([jnp.zeros_like(low[:, :1]), low[:, :-1]], axis=1),
            low,
        )
        high = jnp.where(
            member == groups - 1,
            jnp.concatenate([high[:, 1:], jnp.zeros_like(high[:, :1])], axis=1),
            high,
        )
        return [part.reshape(parts * slot_count, rim_width, -1) for part in (low, high)]

    by_block = normed.reshape(slot_count, blk_rows, model_width)
    before, after = rims(by_block[:, blk_rows - rim_width :], by_block[:, :rim_width], 1)
    normed = jnp.concatenate(
        [normed, before.reshape(-1, model_width), after.reshape(-1, model_width)], axis=0
    )
    normed, columns, dw_weight = lax.optimization_barrier((normed, columns, dw_weight))

    middle = model_width // 2
    y_axes = ("yh", "yl")
    weight_in = [
        columns,
        lax.ppermute(columns[:, :middle], y_axes, ring(y_axes, 1)),
        lax.ppermute(columns[:, middle:], y_axes, ring(y_axes, -1)),
        lax.ppermute(columns, "x", ring("x", -1)),
        lax.ppermute(columns, "x", ring("x", 1)),
    ]
    at = place.reshape(1).astype(jnp.int32)

    other = core_swap(normed)

    extent = groups * slot_count * blk_rows
    offset_rows = jnp.arange(blk_rows + 2 * rim_width, dtype=jnp.int32) - rim_width
    where_at = (position * blk_rows)[:, None] + offset_rows[None, :]

    def labels_of(one):
        bounds = (one[:, :1] * blk_rows + jnp.cumsum(one[:, 1:], axis=1)).reshape(-1)
        found = jnp.sum((bounds[None, None, :] <= where_at[:, :, None]).astype(jnp.int32), axis=-1)
        return jnp.where((where_at >= 0) & (where_at < extent), found, -1)

    labels = jnp.concatenate([labels_of(own_table), labels_of(sib_table)], axis=0)
    labels = jnp.broadcast_to(labels[:, :, None], labels.shape + (LANES,))

    small = jnp.concatenate([dw_weight.reshape(-1, model_width), bn_scale, bn_shift], axis=0)
    small = channels(core.reshape(1).astype(jnp.int32), small, shard)
    tap_rows = layer_count * kernel_taps

    for layer in range(layer_count):
        if layer:
            normed = layer_norm(wide, ln_gain[layer])
            other = core_swap(normed)
        if layer == 0:
            other, labels, small = lax.optimization_barrier((other, labels, small))
        row_of = (layer * kernel_taps, tap_rows + layer, tap_rows + layer_count + layer)

        glu = functools.partial(
            gated_units, slots=slot_count, rim=rim_width, blk=blk_rows, at=at, own=normed, other=other
        )
        glu_one, *rims_one = glu(layer, 0, weights=weight_in[:3])
        if layer:
            rims_two = rims(*rims_one, 2)
            glu_one, weight_out[layer] = lax.optimization_barrier((glu_one, weight_out[layer]))
        glu_two, *edges_two = glu(layer, 1, weights=weight_in[3:])
        if layer:
            rims_one = rims(*edges_two, 2)
            glu_one, glu_two = lax.optimization_barrier((glu_one, glu_two))
            first, second = (1, glu_two, rims_two), (0, glu_one, rims_one)
        else:
            rims_one, rims_two = [
                [part.reshape(2 * slot_count, rim_width, -1) for part in pair]
                for pair in (rims_one, edges_two)
            ]
            first, second = (0, glu_one, rims_one), (1, glu_two, rims_two)
        done = depthwise_call(
            0, 2 * slot_count, kernel_taps, row_of, first[0], at, first[1], *first[2], labels, small
        )
        done, weight_out[layer] = lax.optimization_barrier((done, weight_out[layer]))
        tail = lambda part, kind: depthwise_call(
            part * slot_count, slot_count, kernel_taps, row_of, second[0], at, second[1],
            *second[2], labels, small, (done, weight_out[layer]), kind,
        )
        theirs = core_swap(tail(1, jnp.bfloat16))
        mine = tail(0, jnp.float32)
        update = mine + theirs.astype(jnp.float32)
        frames = (wide + update).astype(jnp.bfloat16)
        wide = frames.astype(jnp.float32)
    return frames


def solution(mesh):
    physical = Mesh(mesh.devices.reshape(SIZES), AXES)
    in_specs = (
        P(DP + GROUP, None, None),
        P(DP, GROUP, None),
        P(DP, GROUP),
        P(),
        P(),
        P(),
        P(),
        P(),
        P(None, DP, None),
        P(),
        P(),
        P(),
        P(None, DP, None),
    )
    out_specs = P(DP + GROUP, None)
    return jax.shard_map(
        local, mesh=physical, in_specs=in_specs, out_specs=out_specs, check_vma=False
    )
```

```python
import functools

import jax
import jax.numpy as jnp
from jax import lax
from jax.experimental import pallas as pl
from jax.experimental.pallas import tpu as pltpu
from jax.sharding import Mesh
from jax.sharding import PartitionSpec as P

FK = 10
TSTRIDE = 4
eps_norm = 1e-05

AXES = ("z", "yh", "c", "yl", "x")
SIZES = (8, 2, 2, 2, 4)
DP = ("z", "yh", "c")
GROUP = ("yl", "x")
LANES = 128
VMEM_LIMIT = 56 * 1024 * 1024
SMALL = pl.CostEstimate(flops=1000, bytes_accessed=1000, transcendentals=0)


def layer_norm(wide, gain):
    centre = wide - jnp.mean(wide, axis=-1, keepdims=True)
    spread = jnp.mean(centre * centre, axis=-1, keepdims=True)
    return (centre * lax.rsqrt(spread + eps_norm) * gain).astype(jnp.bfloat16)


def ring(axis, step):
    count = lax.axis_size(axis)
    return [(i, (i + step) % count) for i in range(count)]


def core_swap(block):
    return lax.ppermute(block, "c", [(0, 1), (1, 0)])


def y_swap(block):
    return lax.ppermute(block, ("yh", "yl"), [(i, 3 - i) for i in range(4)])


def glu_kernel(rim, blk, step, at_ref, own_ref, other_ref, *refs):
    weights, (out_ref, low_ref, high_ref) = refs[:-3], refs[-3:]
    values_first = lax.rem(at_ref[0] + step, 4) < 2
    rows = out_ref.shape[0] // 2
    rim_rows = low_ref.shape[0] // 2

    def product(frames):
        first = jnp.dot(frames, weights[0][...], preferred_element_type=jnp.float32)
        second, depth = 0.0, 0
        for weight in weights[1:]:
            deep = weight.shape[0]
            second = second + jnp.dot(
                frames[:, depth : depth + deep], weight[...], preferred_element_type=jnp.float32
            )
            depth += deep
        a = jnp.where(values_first, first, second)
        b = jnp.where(values_first, second, first)
        return (a * jax.nn.sigmoid(b)).astype(jnp.bfloat16)

    for part, frames_ref in enumerate((own_ref, other_ref)):
        gated = product(frames_ref[...])
        out_ref[part * rows : (part + 1) * rows] = gated[:rows]
        if frames_ref.shape[0] > rows:
            place = slice(part * rim_rows, (part + 1) * rim_rows)
            low_ref[place] = gated[rows : rows + rim_rows]
            high_ref[place] = gated[rows + rim_rows :]
        else:
            for block in range(rows // blk):
                place = part * rim_rows + block * rim
                low_ref[place : place + rim] = gated[(block + 1) * blk - rim : (block + 1) * blk]
                high_ref[place : place + rim] = gated[block * blk : block * blk + rim]


def gated_units(layer, step, rim, blk, slots, at, own, other, weights):
    given, width = own.shape
    cols = weights[0].shape[2]
    rows, rim_rows = slots * blk, slots * rim
    whole = lambda *shape: pl.BlockSpec(shape, lambda i: (0,) * len(shape))
    return pl.pallas_call(
        functools.partial(glu_kernel, rim, blk, step),
        grid=(1,),
        out_shape=[
            jax.ShapeDtypeStruct((2 * count, cols), jnp.bfloat16)
            for count in (rows, rim_rows, rim_rows)
        ],
        in_specs=[pl.BlockSpec(memory_space=pltpu.SMEM), whole(given, width), whole(given, width)]
        + [
            pl.BlockSpec((None,) + w.shape[1:], lambda i, k=min(layer, w.shape[0] - 1): (k, 0, 0))
            for w in weights
        ],
        out_specs=[whole(2 * rows, cols), whole(2 * rim_rows, cols), whole(2 * rim_rows, cols)],
        compiler_params=pltpu.CompilerParams(vmem_limit_bytes=VMEM_LIMIT),
        cost_estimate=SMALL,
        name="gated_units",
    )(at, own, other, *weights)


def channel_kernel(run, core_ref, all_ref, out_ref):
    width, kept = all_ref.shape[1], out_ref.shape[1]
    row = lax.broadcasted_iota(jnp.int32, (width, kept), 0)
    made = lax.broadcasted_iota(jnp.int32, (width, kept), 1)
    taken = (2 * (made // run) + core_ref[0]) * run + made % run
    pick = jnp.where(row == taken, 1.0, 0.0).astype(jnp.bfloat16)
    rest = all_ref[...]
    total = jnp.zeros(out_ref.shape, jnp.float32)
    for _ in range(3):
        piece = rest.astype(jnp.bfloat16)
        total = total + jnp.dot(piece, pick, preferred_element_type=jnp.float32)
        rest = rest - piece.astype(jnp.float32)
    out_ref[...] = total


def channels(core, array, run):
    rows, width = array.shape
    vmem = pl.BlockSpec(memory_space=pltpu.VMEM)
    return pl.pallas_call(
        functools.partial(channel_kernel, run),
        out_shape=jax.ShapeDtypeStruct((rows, width // 2), jnp.float32),
        in_specs=[pl.BlockSpec(memory_space=pltpu.SMEM), vmem],
        out_specs=vmem,
        compiler_params=pltpu.CompilerParams(vmem_limit_bytes=VMEM_LIMIT),
        name="channels",
    )(core, array)


def depthwise(taps, rim, row_of, base, glu_ref, low_ref, high_ref, label_ref, small_ref, padded, store):
    rows, width = glu_ref.shape
    tiles = width // LANES
    for tile in range(tiles):
        lanes = slice(tile * LANES, (tile + 1) * LANES)
        padded[tile, 0:rim] = low_ref[0, :, lanes].astype(jnp.float32)
        padded[tile, rim : rim + rows] = glu_ref[:, lanes].astype(jnp.float32)
        padded[tile, rim + rows : rows + 2 * rim] = high_ref[0, :, lanes].astype(jnp.float32)
    group = 32
    offset = [pl.ds(pl.multiple_of(base + tile * LANES, LANES), LANES) for tile in range(tiles)]
    for start in range(0, rows, group):
        centre = label_ref[0, rim + start : rim + start + group, :]
        totals = [jnp.zeros((group, LANES), jnp.float32)] * tiles
        for tap in range(taps):
            keep = label_ref[0, start + tap : start + tap + group, :] == centre
            for tile in range(tiles):
                window = padded[tile, start + tap : start + tap + group]
                term = window * small_ref[pl.ds(row_of[0] + tap, 1), offset[tile]]
                totals[tile] = totals[tile] + jnp.where(keep, term, 0.0)
        for tile in range(tiles):
            scale = small_ref[pl.ds(row_of[1], 1), offset[tile]]
            shift = small_ref[pl.ds(row_of[2], 1), offset[tile]]
            scaled = totals[tile] * scale + shift
            store(start, group, tile, (scaled * jax.nn.sigmoid(scaled)).astype(jnp.bfloat16))


def depthwise_kernel(taps, rim, row_of, step, at_ref, glu_ref, low_ref, high_ref, label_ref, small_ref, out_ref, padded):
    base = lax.rem(at_ref[0] + step, 2) * glu_ref.shape[1]

    def store(start, group, tile, value):
        out_ref[start : start + group, tile * LANES : (tile + 1) * LANES] = value

    depthwise(
        taps, rim, row_of, base, glu_ref, low_ref, high_ref, label_ref, small_ref, padded, store
    )


def tail_kernel(taps, rim, row_of, step, at_ref, glu_ref, low_ref, high_ref, label_ref, small_ref, done_ref, weight_ref, out_ref, padded, act):
    width = glu_ref.shape[1]
    half = lax.rem(at_ref[0] + step, 2)
    base = half * width

    def store(start, group, tile, value):
        act[start : start + group, tile * LANES : (tile + 1) * LANES] = value

    depthwise(
        taps, rim, row_of, base, glu_ref, low_ref, high_ref, label_ref, small_ref, padded, store
    )
    done_rows = pl.ds(pl.multiple_of((1 - half) * width, width), width)
    here_rows = pl.ds(pl.multiple_of(base, width), width)
    out_ref[...] = (
        jnp.dot(done_ref[...], weight_ref[done_rows, :], preferred_element_type=jnp.float32)
        + jnp.dot(act[...], weight_ref[here_rows, :], preferred_element_type=jnp.float32)
    ).astype(out_ref.dtype)


def depthwise_call(first, count, taps, row_of, step, at, glu, low, high, labels, small, rest=None, kind=None):
    rim, width = low.shape[1:]
    rows = labels.shape[1] - 2 * rim
    whole = lambda *shape: pl.BlockSpec(shape, lambda i: (0,) * len(shape))
    in_specs = [
        pl.BlockSpec(memory_space=pltpu.SMEM),
        pl.BlockSpec((rows, width), lambda i: (first + i, 0)),
        pl.BlockSpec((1, rim, width), lambda i: (first + i, 0, 0)),
        pl.BlockSpec((1, rim, width), lambda i: (first + i, 0, 0)),
        pl.BlockSpec((1, rows + 2 * rim, LANES), lambda i: (first + i, 0, 0)),
        whole(*small.shape),
    ]
    scratch = [pltpu.VMEM((width // LANES, rows + 2 * rim, LANES), jnp.float32)]
    if rest is None:
        body, out_width, kind, more = depthwise_kernel, width, jnp.bfloat16, ()
    else:
        done, weight = rest
        body, out_width, more = tail_kernel, weight.shape[1], (done, weight)
        in_specs += [pl.BlockSpec((rows, width), lambda i: (first + i, 0)), whole(*weight.shape)]
        scratch += [pltpu.VMEM((rows, width), jnp.bfloat16)]
    return pl.pallas_call(
        functools.partial(body, taps, rim, row_of, step),
        grid=(count,),
        out_shape=jax.ShapeDtypeStruct((count * rows, out_width), kind),
        in_specs=in_specs,
        out_specs=pl.BlockSpec((rows, out_width), lambda i: (i, 0)),
        scratch_shapes=scratch,
        compiler_params=pltpu.CompilerParams(vmem_limit_bytes=VMEM_LIMIT),
        cost_estimate=SMALL,
        name="depthwise" if rest is None else "module_tail",
    )(at, glu, low, high, labels, small, *more)


def local(
    feats,
    utt_lengths,
    offsets,
    conv_kernel,
    conv_bias,
    lin_weight,
    lin_bias,
    ln_gain,
    w_in,
    dw_weight,
    bn_scale,
    bn_shift,
    w_out,
):
    groups = lax.axis_size("yl") * lax.axis_size("x")
    member = lax.axis_index(GROUP)
    core = lax.axis_index("c")
    x_at = lax.axis_index("x")
    yh_at = lax.axis_index("yh")
    own_slots = feats.shape[0]
    blk_rows = feats.shape[2]
    slot_count = own_slots // 2
    capacity = (own_slots + groups - 1) // groups
    model_width = lin_weight.shape[1]
    layer_count = ln_gain.shape[0]
    kernel_taps = dw_weight.shape[1]
    rim_width = kernel_taps // 2
    shard = w_in.shape[1]
    half_width = model_width // 2
    y_at = 2 * yh_at + lax.axis_index("yl")

    quarter = 2 * model_width // 4
    place, place_y = [lax.rem(x_at + 2 * (y % 2), 4) for y in (y_at, 3 - y_at)]
    cut = lambda at: lax.dynamic_slice_in_dim(w_in, at * quarter, quarter, axis=2)
    cuts = jnp.concatenate([cut(place), cut(place_y)], axis=0).reshape(-1, quarter)
    made = jnp.arange(quarter, dtype=jnp.int32)
    side, run = made // (quarter // 2), made % (quarter // 2)
    taken = (2 * (run // shard) + jnp.bitwise_xor(side, core)) * shard + run % shard
    pick = (made[:, None] == taken[None, :]).astype(jnp.bfloat16)
    sorted_cuts = jnp.dot(cuts, pick, preferred_element_type=jnp.float32).astype(jnp.bfloat16)
    sorted_cuts = sorted_cuts.reshape(4, shard, 2, quarter // 2)
    mine, sent = sorted_cuts[:, :, 0], sorted_cuts[:, :, 1]
    from_core = core_swap(sent[:2])
    from_y = y_swap(mine[2:])
    from_both = lax.ppermute(sent[2:], ("yh", "c", "yl"), [(i, 7 - i) for i in range(8)])

    def ordered(at, first, second):
        return jnp.where(
            at == 0,
            jnp.concatenate([first, second], axis=1),
            jnp.concatenate([second, first], axis=1),
        )

    both = ordered(
        yh_at, ordered(core, mine[:2], from_core), ordered(core, from_y, from_both)
    )

    feats, utt_lengths, offsets, both = lax.optimization_barrier(
        (feats, utt_lengths, offsets, both)
    )
    columns = lax.all_gather(both, "z", axis=1, tiled=True)

    header = jnp.concatenate([offsets.reshape(1), utt_lengths.reshape(-1)])
    fields = header.shape[0]
    digits = jnp.concatenate([header // 256, header % 256]).astype(feats.dtype)
    head_rows = jnp.zeros((16, blk_rows), feats.dtype).at[0, : 2 * fields].set(digits)
    own_start = offsets.reshape(())
    destined = jnp.arange(groups, dtype=jnp.int32)[:, None]
    rounds = jnp.arange(capacity, dtype=jnp.int32)[None, :]
    chosen = jnp.mod(destined - own_start, groups) + rounds * groups
    outgoing = jnp.concatenate(
        [
            feats[jnp.clip(chosen, 0, own_slots - 1)],
            jnp.broadcast_to(head_rows, chosen.shape + head_rows.shape),
        ],
        axis=2,
    )
    outgoing, w_out = lax.optimization_barrier((outgoing, w_out))
    swapped = y_swap(w_out)
    incoming = lax.all_to_all(outgoing, GROUP, split_axis=0, concat_axis=0, tiled=True)
    incoming, swapped = lax.optimization_barrier((incoming, swapped))

    rows_out = ordered(yh_at, w_out, swapped)
    weight_out = [
        lax.all_gather(rows_out[layer], "z", axis=0, tiled=True) for layer in range(layer_count)
    ]

    raw_rows = feats.shape[1]
    digits = incoming[:, 0, raw_rows, : 2 * fields].astype(jnp.int32)
    own_table = digits[:, :fields] * 256 + digits[:, fields:]
    sib_table = core_swap(own_table)
    starts = own_table[:, 0]
    counts = jnp.sum(own_table[:, 1:], axis=1) // blk_rows
    position = jnp.arange(slot_count, dtype=jnp.int32) * groups + member
    inside = (
        (starts[None, :] <= position[:, None]) & (position[:, None] < (starts + counts)[None, :])
    ).astype(jnp.int32)
    source = jnp.sum(inside * jnp.arange(groups, dtype=jnp.int32)[None, :], axis=1)
    source_start = jnp.sum(inside * starts[None, :], axis=1)
    blocks = incoming[source, (position - source_start) // groups][:, :raw_rows]

    kernel = conv_kernel.reshape(conv_kernel.shape[0], TSTRIDE, FK)
    stacked = blocks.reshape(slot_count, TSTRIDE, -1, FK, blk_rows)
    conv_out = jnp.einsum("cim,bifmt->bcft", kernel, stacked, preferred_element_type=jnp.float32)
    hidden = jax.nn.relu(conv_out + conv_bias[None, :, None, None]).astype(jnp.bfloat16)
    hidden = hidden.reshape(slot_count, -1, blk_rows)
    frames = jnp.einsum("bkt,kd->btd", hidden, lin_weight, preferred_element_type=jnp.float32)
    frames = (frames + lin_bias).astype(jnp.bfloat16).reshape(slot_count * blk_rows, model_width)

    wide = frames.astype(jnp.float32)
    normed = layer_norm(wide, ln_gain[0])

    def rims(last, first, parts):
        low = lax.ppermute(last, GROUP, ring(GROUP, 1)).reshape(parts, slot_count, rim_width, -1)
        high = lax.ppermute(first, GROUP, ring(GROUP, -1)).reshape(parts, slot_count, rim_width, -1)
        low = jnp.where(
            member == 0,
            jnp.concatenate([jnp.zeros_like(low[:, :1]), low[:, :-1]], axis=1),
            low,
        )
        high = jnp.where(
            member == groups - 1,
            jnp.concatenate([high[:, 1:], jnp.zeros_like(high[:, :1])], axis=1),
            high,
        )
        return [part.reshape(parts * slot_count, rim_width, -1) for part in (low, high)]

    by_block = normed.reshape(slot_count, blk_rows, model_width)
    before, after = rims(by_block[:, blk_rows - rim_width :], by_block[:, :rim_width], 1)
    normed = jnp.concatenate(
        [normed, before.reshape(-1, model_width), after.reshape(-1, model_width)], axis=0
    )
    normed, columns, dw_weight = lax.optimization_barrier((normed, columns, dw_weight))

    middle = model_width // 2
    y_axes = ("yh", "yl")
    opposite = [
        columns,
        lax.ppermute(columns[:, :middle], y_axes, ring(y_axes, 1)),
        lax.ppermute(columns[:, middle:], y_axes, ring(y_axes, -1)),
    ]
    sides = lambda held: [lax.ppermute(held, "x", ring("x", step)) for step in (-1, 1)]
    beside = [sides(columns[:1])]
    at = place.reshape(1).astype(jnp.int32)

    other = core_swap(normed)

    extent = groups * slot_count * blk_rows
    offset_rows = jnp.arange(blk_rows + 2 * rim_width, dtype=jnp.int32) - rim_width
    where_at = (position * blk_rows)[:, None] + offset_rows[None, :]

    def labels_of(one):
        bounds = (one[:, :1] * blk_rows + jnp.cumsum(one[:, 1:], axis=1)).reshape(-1)
        found = jnp.sum((bounds[None, None, :] <= where_at[:, :, None]).astype(jnp.int32), axis=-1)
        return jnp.where((where_at >= 0) & (where_at < extent), found, -1)

    labels = jnp.concatenate([labels_of(own_table), labels_of(sib_table)], axis=0)
    labels = jnp.broadcast_to(labels[:, :, None], labels.shape + (LANES,))

    small = jnp.concatenate([dw_weight.reshape(-1, model_width), bn_scale, bn_shift], axis=0)
    small = channels(core.reshape(1).astype(jnp.int32), small, shard)
    tap_rows = layer_count * kernel_taps
    small, later = lax.optimization_barrier((small, columns))
    beside += [sides(later[layer : layer + 1]) for layer in range(1, layer_count)]

    for layer in range(layer_count):
        if layer:
            normed = layer_norm(wide, ln_gain[layer])
            other = core_swap(normed)
        if layer == 0:
            other, labels, small = lax.optimization_barrier((other, labels, small))
        row_of = (layer * kernel_taps, tap_rows + layer, tap_rows + layer_count + layer)

        glu = functools.partial(
            gated_units, slots=slot_count, rim=rim_width, blk=blk_rows, at=at, own=normed, other=other
        )
        if layer:
            glu_one, *edges_one = glu(layer, 0, weights=opposite)
            rims_two = rims(*edges_one, 2)
            glu_one, weight_out[layer] = lax.optimization_barrier((glu_one, weight_out[layer]))
            glu_two, *edges_two = glu(layer, 1, weights=beside[layer])
            rims_one = rims(*edges_two, 2)
            glu_one, glu_two = lax.optimization_barrier((glu_one, glu_two))
            first, second = (1, glu_two, rims_two), (0, glu_one, rims_one)
        else:
            glu_two, *rims_two = glu(layer, 1, weights=beside[layer])
            glu_two, opposite = lax.optimization_barrier((glu_two, opposite))
            glu_one, *rims_one = glu(layer, 0, weights=opposite)
            rims_one, rims_two = [
                [part.reshape(2 * slot_count, rim_width, -1) for part in pair]
                for pair in (rims_one, rims_two)
            ]
            first, second = (1, glu_two, rims_two), (0, glu_one, rims_one)
        done = depthwise_call(
            0, 2 * slot_count, kernel_taps, row_of, first[0], at, first[1], *first[2], labels, small
        )
        done, weight_out[layer] = lax.optimization_barrier((done, weight_out[layer]))
        tail = lambda part, kind: depthwise_call(
            part * slot_count, slot_count, kernel_taps, row_of, second[0], at, second[1],
            *second[2], labels, small, (done, weight_out[layer]), kind,
        )
        partial = tail(1, jnp.bfloat16)
        theirs = core_swap(partial)
        if layer + 1 < layer_count:
            partial, beside[layer + 1], done = lax.optimization_barrier(
                (partial, beside[layer + 1], done)
            )
        mine = tail(0, jnp.float32)
        update = mine + theirs.astype(jnp.float32)
        frames = (wide + update).astype(jnp.bfloat16)
        wide = frames.astype(jnp.float32)
    return frames


def solution(mesh):
    physical = Mesh(mesh.devices.reshape(SIZES), AXES)
    in_specs = (
        P(DP + GROUP, None, None),
        P(DP, GROUP, None),
        P(DP, GROUP),
        P(),
        P(),
        P(),
        P(),
        P(),
        P(None, DP, None),
        P(),
        P(),
        P(),
        P(None, DP, None),
    )
    out_specs = P(DP + GROUP, None)
    return jax.shard_map(
        local, mesh=physical, in_specs=in_specs, out_specs=out_specs, check_vma=False
    )
```
